32 devices in a mesh: tm: 8 (over z, y), pix: 4 (over x, core).
Axes of the slice: x: 2, y: 2, z: 4, core: 2. Of those that a mesh axis runs over, the one named last changes fastest.
Arguments:
- frames: bfloat16 [1024, 131072], P('tm', 'pix'), may hold values from -30 to 30, as said below
- band_edges: int32 [65], replicated, may hold values from 0 to 384, as said below
Outputs:
- coherence: float32 [64, 2, 8, 8], P('tm')
The draws below stay inside these ranges and needn't reach their ends.
Inputs may be any that keep to these rules, and one draw needn't show every extreme that they name: `frames`: image intensities with a level of their own in each pixel. Strictly increasing, band_edges[0] = 0 and band_edges[64] = 384; the bands have uneven widths.
All inputs are finite; a program needn't handle non-finite values.
Results may differ from the reference program's by a relative error of at most 0.0096.
Values may be sent and summed in bfloat16 or wider, within the bound.
A program may use at most 192 MiB of HBM per device.

```python
import math
import jax
import jax.numpy as jnp
from jax import lax

NT = 1024
TAPERS = 8
NB = 384
NBANDS = 64
PIX_DEV = 32768
PIXELS = 131072
N_PIX = 4


def draw_frames(key, part):
    noise_key = jax.random.fold_in(key, 11)
    scale_key = jax.random.fold_in(key, 12)
    level_key = jax.random.fold_in(key, 13)
    noise_part = jnp.clip(jax.random.normal(noise_key, (NT, PIXELS), jnp.float32), -6.0, 6.0)
    scaling = jnp.exp(jax.random.uniform(scale_key, (1, PIXELS), jnp.float32, -0.7, 0.7))
    offset = jax.random.uniform(level_key, (1, PIXELS), jnp.float32, -1.0, 1.0)
    return ((noise_part + offset) * scaling).astype(jnp.bfloat16)


def draw_band_edges(key, part):
    cut_points = jax.random.permutation(jax.random.fold_in(key, 21), NB - 1)[:NBANDS - 1].astype(jnp.int32) + 1
    cut_points = jnp.sort(cut_points)
    return jnp.concatenate([jnp.zeros((1,), jnp.int32), cut_points, jnp.full((1,), NB, jnp.int32)])


def setup_inputs(seed: int = 0) -> dict:
    keys = jax.random.split(jax.random.key(seed), 3)
    return {
        "frames": draw_frames(jax.random.fold_in(keys[2], 71), 0),
        "band_edges": draw_band_edges(jax.random.fold_in(keys[2], 71), 0),
    }


def transform_table(length, bins, tapers):
    frame_ids = jnp.arange(length, dtype=jnp.int32)
    bin_ids = jnp.arange(bins, dtype=jnp.int32)
    phase = (bin_ids[:, None] * frame_ids[None, :] % length).astype(jnp.float32) * (2.0 * math.pi / length)
    orders = jnp.arange(1, tapers + 1, dtype=jnp.int32).astype(jnp.float32)
    taper_rows = math.sqrt(2.0 / (length + 1)) * jnp.sin(math.pi * orders[:, None] * (frame_ids[None, :].astype(jnp.float32) + 1.0) / (length + 1))
    real_part = taper_rows[:, None, :] * jnp.cos(phase)[None]
    imag_part = -taper_rows[:, None, :] * jnp.sin(phase)[None]
    dft_table = jnp.stack([real_part, imag_part], axis=1)
    return dft_table.reshape(tapers * 2 * bins, length).astype(jnp.bfloat16)

def bin_cross(spectra, tapers, bins):
    rows_by_part = spectra.reshape(2 * tapers, bins, -1)
    per_bin = jnp.einsum('afp,bfp->fab', rows_by_part, rows_by_part, precision=lax.Precision.HIGHEST)
    return per_bin.reshape(bins, 4 * tapers * tapers)

def band_matrix(band_edges, bins):
    bin_ids = jnp.arange(bins, dtype=jnp.int32)
    band_mask = (bin_ids[None, :] >= band_edges[:-1, None]) & (bin_ids[None, :] < band_edges[1:, None])
    return band_mask.astype(jnp.float32)

def coherence_of(band_sums, counts, total_pixels, tapers):
    blocks = band_sums.reshape(-1, tapers, 2, tapers, 2)
    real_part = blocks[:, :, 0, :, 0] + blocks[:, :, 1, :, 1]
    imag_part = blocks[:, :, 1, :, 0] - blocks[:, :, 0, :, 1]
    power_diag = jnp.diagonal(real_part, axis1=1, axis2=2) + 1e-06
    denominator = jnp.sqrt(power_diag[:, :, None] * power_diag[:, None, :])
    scaling = jnp.sqrt(counts * jnp.float32(total_pixels))[:, None, None]
    off_diagonal = 1.0 - jnp.eye(tapers, dtype=jnp.float32)
    factor = scaling * off_diagonal / denominator
    return jnp.stack([real_part * factor, imag_part * factor], axis=1)

def centered_spectra(pixel_block, dft_table):
    widened = pixel_block.astype(jnp.float32)
    frame_mean = lax.optimization_barrier(jnp.mean(widened, axis=0, keepdims=True))
    centered = (widened - frame_mean).astype(jnp.bfloat16)
    return jnp.dot(dft_table.astype(jnp.float32), centered.astype(jnp.float32))

def reference(frames, band_edges):
    dft_table = transform_table(NT, NB, TAPERS)
    pixel_blocks = frames.reshape(NT, N_PIX * 8, PIX_DEV // 8).transpose(1, 0, 2)

    def accumulate(running, pixel_block):
        spectra = centered_spectra(pixel_block, dft_table)
        return (running + bin_cross(spectra, TAPERS, NB), None)
    running, _ = lax.scan(accumulate, jnp.zeros((NB, 4 * TAPERS * TAPERS), jnp.float32), pixel_blocks)
    band_mask = band_matrix(band_edges, NB)
    band_sums = jnp.dot(band_mask, running, precision=lax.Precision.HIGHEST)
    counts = lax.optimization_barrier(jnp.sum(band_mask, axis=1))
    return coherence_of(band_sums, counts, PIXELS, TAPERS)
```

```python
import functools
import math

import jax
import jax.numpy as jnp
import ml_dtypes
import numpy as np
from jax import lax
from jax.experimental import pallas as pl
from jax.experimental.pallas import tpu as pltpu
from jax.sharding import PartitionSpec as P

TAPERS = 8
NB = 384
NBANDS = 64
PAIRS = TAPERS * TAPERS
BINS = 8
TILE = 256
CHUNK = 256
GROUP = 2 * TAPERS * BINS
GROUPS = NB // BINS
ROWS = 1024
MESH = pl.DeviceIdType.MESH
HIGHEST = lax.Precision.HIGHEST


def tables(length):
    frames = np.arange(length)
    phase = (np.arange(NB)[:, None] * frames[None, :] % length) * (2.0 * math.pi / length)
    trig = np.stack([np.cos(phase), -np.sin(phase)]).reshape(2, GROUPS, BINS, length)
    trig = trig.transpose(1, 0, 2, 3).reshape(2 * NB, length).astype(np.float32)
    rate = np.pi * (np.arange(TAPERS) + 1.0) / (length + 1)
    tapers = math.sqrt(2.0 / (length + 1)) * np.sin(rate[:, None] * (frames + 1.0))
    combine = np.zeros((2 * TAPERS, 2 * TAPERS, BINS, 2 * PAIRS), np.float32)
    power = np.zeros((2 * PAIRS, 2, 2, TAPERS, TAPERS), np.float32)
    for k in range(TAPERS):
        for l in range(TAPERS):
            kl = k * TAPERS + l
            combine[2 * k, 2 * l, :, kl] = 1.0
            combine[2 * k + 1, 2 * l + 1, :, kl] = 1.0
            combine[2 * k + 1, 2 * l, :, PAIRS + kl] = 1.0
            combine[2 * k, 2 * l + 1, :, PAIRS + kl] = -1.0
            power[k * TAPERS + k, 0, :, k, l] = 1.0
            power[l * TAPERS + l, 1, :, k, l] = 1.0
    combine = combine.reshape(2 * TAPERS * GROUP, 2 * PAIRS).astype(ml_dtypes.bfloat16)
    return trig, tapers.astype(np.float32), combine, power.reshape(2 * PAIRS, 4 * PAIRS)


def split(value):
    high = value.astype(jnp.bfloat16)
    return high, (value - high.astype(jnp.float32)).astype(jnp.bfloat16)


def kernel(
    groups, pixes, total_pixels,
    edges_ref, frames_ref, trig_hbm, tapers_hbm, combine_hbm, power_hbm,
    out_ref,
    data, centered, table, cross, trig, tapers, combine, power, mask, counts,
    part, got_tm, share, got_pix,
    table_sem, local_sem, send_sem, recv_sem, send_tm, recv_tm, send_pix, recv_pix,
):
    me = lax.axis_index("tm")
    me_pix = lax.axis_index("pix")
    chunks, frame_total, cols = data.shape
    frames_dev = frame_total // groups
    share_cols = chunks * cols
    own_bands = NBANDS // groups
    tiles = frame_total // TILE
    steps = sorted(range(1, groups), key=lambda d: (abs(d - groups // 2), d))

    def rows_of(group):
        return pl.ds(pl.multiple_of(group * frames_dev, frames_dev), frames_dev)

    def columns_of(group, s):
        return pl.ds(pl.multiple_of(group * share_cols + s * cols, 128), cols)

    barrier = pltpu.get_barrier_semaphore()
    for d in range(1, groups):
        pl.semaphore_signal(
            barrier, inc=1, device_id=(lax.rem(me + d, groups), me_pix), device_id_type=MESH
        )
    for d in range(1, pixes):
        pl.semaphore_signal(
            barrier, inc=1, device_id=(me, lax.rem(me_pix + d, pixes)), device_id_type=MESH
        )
    pl.semaphore_wait(barrier, groups - 1 + pixes - 1)

    def frame_copy(s, d):
        to = lax.rem(me + d, groups)
        return pltpu.make_async_remote_copy(
            src_ref=frames_ref.at[:, columns_of(to, s)],
            dst_ref=data.at[s, rows_of(me), :],
            send_sem=send_sem.at[s, d],
            recv_sem=recv_sem.at[s, d],
            device_id=(to, me_pix),
            device_id_type=MESH,
        )

    def own_copy(s):
        return pltpu.make_async_copy(
            frames_ref.at[:, columns_of(me, s)], data.at[s, rows_of(me), :], local_sem.at[s]
        )

    def send(s, carry):
        for d in steps:
            frame_copy(s, d).start()
        own_copy(s).start()
        return carry

    lax.fori_loop(0, chunks, send, 0)

    table_copies = [
        pltpu.make_async_copy(source, target, table_sem.at[i])
        for i, (source, target) in enumerate(
            [(trig_hbm, trig), (tapers_hbm, tapers), (combine_hbm, combine), (power_hbm, power)]
        )
    ]
    for copy in table_copies:
        copy.start()

    bin_ids = lax.broadcasted_iota(jnp.int32, (1, NB), 1)
    for b in range(NBANDS):
        inside = (bin_ids >= edges_ref[b]) & (bin_ids < edges_ref[b + 1])
        mask[b:b + 1, :] = jnp.where(inside, 1.0, 0.0)
        count = (edges_ref[b + 1] - edges_ref[b]).astype(jnp.float32)
        counts[b // own_bands, b % own_bands:b % own_bands + 1, :] = jnp.full(
            (1, 2 * PAIRS), count, jnp.float32
        )
    for copy in table_copies:
        copy.wait()
    cross[...] = jnp.zeros_like(cross)

    def fill(g, carry):
        waves = trig[pl.ds(pl.multiple_of(g * 2 * BINS, 2 * BINS), 2 * BINS), :]
        for k in range(TAPERS):
            rows = pl.ds(pl.multiple_of(g * GROUP + k * 2 * BINS, 2 * BINS), 2 * BINS)
            table[rows, :] = (waves * tapers[k:k + 1, :]).astype(jnp.bfloat16)
        return carry

    lax.fori_loop(0, GROUPS, fill, 0)

    def accumulate(s, carry):
        own_copy(s).wait()
        for d in steps:
            source = lax.rem(me + groups - d, groups)
            pltpu.make_async_remote_copy(
                src_ref=frames_ref.at[:, columns_of(me, s)],
                dst_ref=data.at[s, rows_of(source), :],
                send_sem=send_sem.at[s, d],
                recv_sem=recv_sem.at[s, d],
                device_id=(source, me_pix),
                device_id_type=MESH,
            ).wait_recv()
        total = jnp.zeros((1, cols), jnp.float32)
        for i in range(tiles):
            block = data[s, i * TILE:(i + 1) * TILE, :].astype(jnp.float32)
            total = total + jnp.sum(block, axis=0, keepdims=True)
        mean = total * (1.0 / frame_total)
        for i in range(tiles):
            block = data[s, i * TILE:(i + 1) * TILE, :].astype(jnp.float32)
            block = (block - mean).astype(jnp.bfloat16)
            centered[i * TILE:(i + 1) * TILE, :] = block

        def transform(r, inner):
            rows = pl.ds(pl.multiple_of(r * ROWS, ROWS), ROWS)
            spectra = jnp.dot(
                table[rows, :], centered[...], preferred_element_type=jnp.float32
            ).astype(jnp.bfloat16)
            for g in range(ROWS // GROUP):
                block = spectra[g * GROUP:(g + 1) * GROUP]
                cross[r * (ROWS // GROUP) + g] += lax.dot_general(
                    block, block, (((1,), (1,)), ((), ())), preferred_element_type=jnp.float32
                )
            return inner

        return lax.fori_loop(0, GROUPS * GROUP // ROWS, transform, carry)

    lax.fori_loop(0, chunks, accumulate, 0)

    band_mask = mask[...].astype(jnp.bfloat16)
    same_bin = (
        lax.broadcasted_iota(jnp.int32, (BINS, GROUP), 1) % BINS
        == lax.broadcasted_iota(jnp.int32, (BINS, GROUP), 0)
    )
    pieces = []
    for a in range(0, 2 * TAPERS, 2):
        sides = []
        for row in (a, a + 1):
            side = jnp.where(same_bin[None], cross[:, row * BINS:(row + 1) * BINS, :], 0.0)
            sides.append(side.reshape(NB, GROUP))
        high, low = split(jnp.concatenate(sides, axis=1))
        pieces.append(
            jnp.dot(band_mask, high, preferred_element_type=jnp.float32)
            + jnp.dot(band_mask, low, preferred_element_type=jnp.float32)
        )
    high, low = split(jnp.concatenate(pieces, axis=1))
    both = jnp.dot(
        jnp.concatenate([high, low], axis=0), combine[...], preferred_element_type=jnp.float32
    )
    both = both[:NBANDS] + both[NBANDS:]
    for g in range(groups):
        part[g] = both[g * own_bands:(g + 1) * own_bands, :]

    def band_copy(d, target, slot):
        return pltpu.make_async_remote_copy(
            src_ref=part.at[target],
            dst_ref=got_tm.at[slot],
            send_sem=send_tm.at[d],
            recv_sem=recv_tm.at[d],
            device_id=(target, me_pix),
            device_id_type=MESH,
        )

    for d in steps:
        band_copy(d, lax.rem(me + d, groups), me).start()
    got_tm[me] = part[me]
    for d in steps:
        source = lax.rem(me + groups - d, groups)
        band_copy(d, source, source).wait_recv()
    value = got_tm[0]
    for g in range(1, groups):
        value = value + got_tm[g]
    share[...] = value
    got_pix[me_pix] = value

    def share_copy(d, target, slot):
        return pltpu.make_async_remote_copy(
            src_ref=share,
            dst_ref=got_pix.at[slot],
            send_sem=send_pix.at[d],
            recv_sem=recv_pix.at[d],
            device_id=(me, target),
            device_id_type=MESH,
        )

    for d in range(1, pixes):
        share_copy(d, lax.rem(me_pix + d, pixes), me_pix).start()
    for d in range(1, pixes):
        source = lax.rem(me_pix + pixes - d, pixes)
        share_copy(d, source, source).wait_recv()
    value = got_pix[0]
    for g in range(1, pixes):
        value = value + got_pix[g]

    powers = jnp.dot(value, power[...], precision=HIGHEST, preferred_element_type=jnp.float32)
    power_k = powers[:, :2 * PAIRS] + 1e-6
    power_l = powers[:, 2 * PAIRS:] + 1e-6
    lane = lax.broadcasted_iota(jnp.int32, value.shape, 1) % PAIRS
    off_diagonal = jnp.where(lane // TAPERS == lane % TAPERS, 0.0, 1.0)
    scaling = jnp.sqrt(counts[me] * total_pixels)
    out_ref[...] = value * (scaling * off_diagonal / jnp.sqrt(power_k * power_l))

    def drain(s, carry):
        for d in steps:
            frame_copy(s, d).wait_send()
        return carry

    lax.fori_loop(0, chunks, drain, 0)
    for d in steps:
        band_copy(d, lax.rem(me + d, groups), me).wait_send()
    for d in range(1, pixes):
        share_copy(d, lax.rem(me_pix + d, pixes), me_pix).wait_send()


def local(frames, band_edges):
    groups = lax.axis_size("tm")
    pixes = lax.axis_size("pix")
    frames_dev, pix_dev = frames.shape
    frame_total = frames_dev * groups
    share_cols = pix_dev // groups
    cols = min(CHUNK, share_cols)
    chunks = share_cols // cols
    own_bands = NBANDS // groups
    trig, tapers, combine, power = tables(frame_total)
    anywhere = pl.BlockSpec(memory_space=pl.ANY)
    lanes = 2 * PAIRS
    result = pl.pallas_call(
        functools.partial(kernel, groups, pixes, float(pix_dev * pixes)),
        out_shape=jax.ShapeDtypeStruct((own_bands, lanes), jnp.float32),
        in_specs=[pl.BlockSpec(memory_space=pltpu.SMEM)] + [anywhere] * 5,
        out_specs=pl.BlockSpec(memory_space=pltpu.VMEM),
        scratch_shapes=[
            pltpu.VMEM((chunks, frame_total, cols), jnp.bfloat16),
            pltpu.VMEM((frame_total, cols), jnp.bfloat16),
            pltpu.VMEM((GROUPS * GROUP, frame_total), jnp.bfloat16),
            pltpu.VMEM((GROUPS, GROUP, GROUP), jnp.float32),
            pltpu.VMEM(trig.shape, jnp.float32),
            pltpu.VMEM(tapers.shape, jnp.float32),
            pltpu.VMEM(combine.shape, jnp.bfloat16),
            pltpu.VMEM(power.shape, jnp.float32),
            pltpu.VMEM((NBANDS, NB), jnp.float32),
            pltpu.VMEM((groups, own_bands, lanes), jnp.float32),
            pltpu.VMEM((groups, own_bands, lanes), jnp.float32),
            pltpu.VMEM((groups, own_bands, lanes), jnp.float32),
            pltpu.VMEM((own_bands, lanes), jnp.float32),
            pltpu.VMEM((pixes, own_bands, lanes), jnp.float32),
            pltpu.SemaphoreType.DMA((4,)),
            pltpu.SemaphoreType.DMA((chunks,)),
            pltpu.SemaphoreType.DMA((chunks, groups)),
            pltpu.SemaphoreType.DMA((chunks, groups)),
            pltpu.SemaphoreType.DMA((groups,)),
            pltpu.SemaphoreType.DMA((groups,)),
            pltpu.SemaphoreType.DMA((pixes,)),
            pltpu.SemaphoreType.DMA((pixes,)),
        ],
        compiler_params=pltpu.CompilerParams(
            collective_id=0, has_side_effects=True, vmem_limit_bytes=56 * 2**20
        ),
        cost_estimate=pl.CostEstimate(
            flops=2 * GROUPS * GROUP * frame_total * share_cols,
            bytes_accessed=4 * frame_total * share_cols,
            transcendentals=0,
        ),
        name="band_coherence",
    )(band_edges, frames, trig, tapers, combine, power)
    return result.reshape(own_bands, 2, TAPERS, TAPERS)


def solution(mesh):
    return jax.shard_map(
        local,
        mesh=mesh,
        in_specs=(P("tm", "pix"), P()),
        out_specs=P("tm", None, None, None),
        check_vma=False,
    )
```

```python
import functools
import math

import jax
import jax.numpy as jnp
import ml_dtypes
import numpy as np
from jax import lax
from jax.experimental import pallas as pl
from jax.experimental.pallas import tpu as pltpu
from jax.sharding import PartitionSpec as P

TAPERS = 8
NB = 384
NBANDS = 64
PAIRS = TAPERS * TAPERS
BINS = 8
TILE = 256
CHUNK = 256
GROUP = 2 * TAPERS * BINS
GROUPS = NB // BINS
ROWS = 1024
MESH = pl.DeviceIdType.MESH
HIGHEST = lax.Precision.HIGHEST


def tables(length):
    frames = np.arange(length)
    phase = (np.arange(NB)[:, None] * frames[None, :] % length) * (2.0 * math.pi / length)
    trig = np.stack([np.cos(phase), -np.sin(phase)]).reshape(2, GROUPS, BINS, length)
    trig = trig.transpose(1, 0, 2, 3).reshape(2 * NB, length).astype(np.float32)
    rate = np.pi * (np.arange(TAPERS) + 1.0) / (length + 1)
    tapers = math.sqrt(2.0 / (length + 1)) * np.sin(rate[:, None] * (frames + 1.0))
    combine = np.zeros((2 * TAPERS, 2 * TAPERS, BINS, 2 * PAIRS), np.float32)
    power = np.zeros((2 * PAIRS, 2, 2, TAPERS, TAPERS), np.float32)
    for k in range(TAPERS):
        for l in range(TAPERS):
            kl = k * TAPERS + l
            combine[2 * k, 2 * l, :, kl] = 1.0
            combine[2 * k + 1, 2 * l + 1, :, kl] = 1.0
            combine[2 * k + 1, 2 * l, :, PAIRS + kl] = 1.0
            combine[2 * k, 2 * l + 1, :, PAIRS + kl] = -1.0
            power[k * TAPERS + k, 0, :, k, l] = 1.0
            power[l * TAPERS + l, 1, :, k, l] = 1.0
    combine = combine.reshape(2 * TAPERS * GROUP, 2 * PAIRS).astype(ml_dtypes.bfloat16)
    return trig, tapers.astype(np.float32), combine, power.reshape(2 * PAIRS, 4 * PAIRS)


def split(value):
    high = value.astype(jnp.bfloat16)
    return high, (value - high.astype(jnp.float32)).astype(jnp.bfloat16)


def kernel(
    groups, pixes, total_pixels,
    edges_ref, frames_ref, trig_hbm, tapers_hbm, combine_hbm, power_hbm,
    out_ref,
    data, centered, table, cross, trig, tapers, combine, power, mask, counts,
    part, got_tm, share, got_pix,
    table_sem, local_sem, send_sem, recv_sem, send_tm, recv_tm, send_pix, recv_pix,
):
    me = lax.axis_index("tm")
    me_pix = lax.axis_index("pix")
    chunks, frame_total, cols = data.shape
    frames_dev = frame_total // groups
    share_cols = chunks * cols
    own_bands = NBANDS // groups
    tiles = frame_total // TILE
    half = groups // 2
    base = me // half * half
    mine = me - base
    across = list(range(half))
    beside = list(range(half + 1, groups))
    peers = across + beside

    def target_of(d):
        return (half - base if d < half else base) + lax.rem(mine + d, half)

    def source_of(d):
        return (half - base if d < half else base) + lax.rem(mine + groups - d, half)

    def rows_of(group):
        return pl.ds(pl.multiple_of(group * frames_dev, frames_dev), frames_dev)

    def columns_of(group, s):
        return pl.ds(pl.multiple_of(group * share_cols + s * cols, 128), cols)

    barrier = pltpu.get_barrier_semaphore()
    for d in peers:
        pl.semaphore_signal(
            barrier, inc=1, device_id=(target_of(d), me_pix), device_id_type=MESH
        )
    for d in range(1, pixes):
        pl.semaphore_signal(
            barrier, inc=1, device_id=(me, lax.rem(me_pix + d, pixes)), device_id_type=MESH
        )
    pl.semaphore_wait(barrier, groups - 1 + pixes - 1)

    def frame_copy(s, d):
        to = target_of(d)
        return pltpu.make_async_remote_copy(
            src_ref=frames_ref.at[:, columns_of(to, s)],
            dst_ref=data.at[s, rows_of(me), :],
            send_sem=send_sem.at[s, d],
            recv_sem=recv_sem.at[s, d],
            device_id=(to, me_pix),
            device_id_type=MESH,
        )

    def own_copy(s):
        return pltpu.make_async_copy(
            frames_ref.at[:, columns_of(me, s)], data.at[s, rows_of(me), :], local_sem.at[s]
        )

    def send(s, carry):
        for d in across:
            frame_copy(s, d).start()
        for near in (2 * s, 2 * s + 1):
            for d in beside:
                frame_copy(near, d).start()
            own_copy(near).start()
        return carry

    def send_across(s, carry):
        for d in across:
            frame_copy(s, d).start()
        return carry

    lax.fori_loop(0, chunks // 2, send, 0)
    lax.fori_loop(chunks // 2, chunks, send_across, 0)

    table_copies = [
        pltpu.make_async_copy(source, target, table_sem.at[i])
        for i, (source, target) in enumerate(
            [(trig_hbm, trig), (tapers_hbm, tapers), (combine_hbm, combine), (power_hbm, power)]
        )
    ]
    for copy in table_copies:
        copy.start()

    bin_ids = lax.broadcasted_iota(jnp.int32, (1, NB), 1)
    for b in range(NBANDS):
        inside = (bin_ids >= edges_ref[b]) & (bin_ids < edges_ref[b + 1])
        mask[b:b + 1, :] = jnp.where(inside, 1.0, 0.0)
        count = (edges_ref[b + 1] - edges_ref[b]).astype(jnp.float32)
        counts[b // own_bands, b % own_bands:b % own_bands + 1, :] = jnp.full(
            (1, 2 * PAIRS), count, jnp.float32
        )
    for copy in table_copies:
        copy.wait()
    cross[...] = jnp.zeros_like(cross)

    def fill(g, carry):
        waves = trig[pl.ds(pl.multiple_of(g * 2 * BINS, 2 * BINS), 2 * BINS), :]
        for k in range(TAPERS):
            rows = pl.ds(pl.multiple_of(g * GROUP + k * 2 * BINS, 2 * BINS), 2 * BINS)
            table[rows, :] = (waves * tapers[k:k + 1, :]).astype(jnp.bfloat16)
        return carry

    lax.fori_loop(0, GROUPS, fill, 0)

    def accumulate(s, carry):
        own_copy(s).wait()
        for d in peers:
            source = source_of(d)
            pltpu.make_async_remote_copy(
                src_ref=frames_ref.at[:, columns_of(me, s)],
                dst_ref=data.at[s, rows_of(source), :],
                send_sem=send_sem.at[s, d],
                recv_sem=recv_sem.at[s, d],
                device_id=(source, me_pix),
                device_id_type=MESH,
            ).wait_recv()
        total = jnp.zeros((1, cols), jnp.float32)
        for i in range(tiles):
            block = data[s, i * TILE:(i + 1) * TILE, :].astype(jnp.float32)
            total = total + jnp.sum(block, axis=0, keepdims=True)
        mean = total * (1.0 / frame_total)
        for i in range(tiles):
            block = data[s, i * TILE:(i + 1) * TILE, :].astype(jnp.float32)
            block = (block - mean).astype(jnp.bfloat16)
            centered[i * TILE:(i + 1) * TILE, :] = block

        def transform(r, inner):
            rows = pl.ds(pl.multiple_of(r * ROWS, ROWS), ROWS)
            spectra = jnp.dot(
                table[rows, :], centered[...], preferred_element_type=jnp.float32
            ).astype(jnp.bfloat16)
            for g in range(ROWS // GROUP):
                block = spectra[g * GROUP:(g + 1) * GROUP]
                cross[r * (ROWS // GROUP) + g] += lax.dot_general(
                    block, block, (((1,), (1,)), ((), ())), preferred_element_type=jnp.float32
                )
            return inner

        return lax.fori_loop(0, GROUPS * GROUP // ROWS, transform, carry)

    lax.fori_loop(0, chunks, accumulate, 0)

    band_mask = mask[...].astype(jnp.bfloat16)
    same_bin = (
        lax.broadcasted_iota(jnp.int32, (BINS, GROUP), 1) % BINS
        == lax.broadcasted_iota(jnp.int32, (BINS, GROUP), 0)
    )
    pieces = []
    for a in range(0, 2 * TAPERS, 2):
        sides = []
        for row in (a, a + 1):
            side = jnp.where(same_bin[None], cross[:, row * BINS:(row + 1) * BINS, :], 0.0)
            sides.append(side.reshape(NB, GROUP))
        high, low = split(jnp.concatenate(sides, axis=1))
        pieces.append(
            jnp.dot(band_mask, high, preferred_element_type=jnp.float32)
            + jnp.dot(band_mask, low, preferred_element_type=jnp.float32)
        )
    high, low = split(jnp.concatenate(pieces, axis=1))
    both = jnp.dot(
        jnp.concatenate([high, low], axis=0), combine[...], preferred_element_type=jnp.float32
    )
    both = both[:NBANDS] + both[NBANDS:]
    for g in range(groups):
        part[g] = both[g * own_bands:(g + 1) * own_bands, :]

    def band_copy(d, target, slot):
        return pltpu.make_async_remote_copy(
            src_ref=part.at[target],
            dst_ref=got_tm.at[slot],
            send_sem=send_tm.at[d],
            recv_sem=recv_tm.at[d],
            device_id=(target, me_pix),
            device_id_type=MESH,
        )

    for d in peers:
        band_copy(d, target_of(d), me).start()
    got_tm[me] = part[me]
    for d in peers:
        source = source_of(d)
        band_copy(d, source, source).wait_recv()
    value = got_tm[0]
    for g in range(1, groups):
        value = value + got_tm[g]
    share[...] = value
    got_pix[me_pix] = value

    def share_copy(d, target, slot):
        return pltpu.make_async_remote_copy(
            src_ref=share,
            dst_ref=got_pix.at[slot],
            send_sem=send_pix.at[d],
            recv_sem=recv_pix.at[d],
            device_id=(me, target),
            device_id_type=MESH,
        )

    for d in range(1, pixes):
        share_copy(d, lax.rem(me_pix + d, pixes), me_pix).start()
    for d in range(1, pixes):
        source = lax.rem(me_pix + pixes - d, pixes)
        share_copy(d, source, source).wait_recv()
    value = got_pix[0]
    for g in range(1, pixes):
        value = value + got_pix[g]

    powers = jnp.dot(value, power[...], precision=HIGHEST, preferred_element_type=jnp.float32)
    power_k = powers[:, :2 * PAIRS] + 1e-6
    power_l = powers[:, 2 * PAIRS:] + 1e-6
    lane = lax.broadcasted_iota(jnp.int32, value.shape, 1) % PAIRS
    off_diagonal = jnp.where(lane // TAPERS == lane % TAPERS, 0.0, 1.0)
    scaling = jnp.sqrt(counts[me] * total_pixels)
    out_ref[...] = value * (scaling * off_diagonal / jnp.sqrt(power_k * power_l))

    def drain(s, carry):
        for d in peers:
            frame_copy(s, d).wait_send()
        return carry

    lax.fori_loop(0, chunks, drain, 0)
    for d in peers:
        band_copy(d, target_of(d), me).wait_send()
    for d in range(1, pixes):
        share_copy(d, lax.rem(me_pix + d, pixes), me_pix).wait_send()


def local(frames, band_edges):
    groups = lax.axis_size("tm")
    pixes = lax.axis_size("pix")
    frames_dev, pix_dev = frames.shape
    frame_total = frames_dev * groups
    share_cols = pix_dev // groups
    cols = min(CHUNK, share_cols)
    chunks = share_cols // cols
    own_bands = NBANDS // groups
    trig, tapers, combine, power = tables(frame_total)
    anywhere = pl.BlockSpec(memory_space=pl.ANY)
    lanes = 2 * PAIRS
    result = pl.pallas_call(
        functools.partial(kernel, groups, pixes, float(pix_dev * pixes)),
        out_shape=jax.ShapeDtypeStruct((own_bands, lanes), jnp.float32),
        in_specs=[pl.BlockSpec(memory_space=pltpu.SMEM)] + [anywhere] * 5,
        out_specs=pl.BlockSpec(memory_space=pltpu.VMEM),
        scratch_shapes=[
            pltpu.VMEM((chunks, frame_total, cols), jnp.bfloat16),
            pltpu.VMEM((frame_total, cols), jnp.bfloat16),
            pltpu.VMEM((GROUPS * GROUP, frame_total), jnp.bfloat16),
            pltpu.VMEM((GROUPS, GROUP, GROUP), jnp.float32),
            pltpu.VMEM(trig.shape, jnp.float32),
            pltpu.VMEM(tapers.shape, jnp.float32),
            pltpu.VMEM(combine.shape, jnp.bfloat16),
            pltpu.VMEM(power.shape, jnp.float32),
            pltpu.VMEM((NBANDS, NB), jnp.float32),
            pltpu.VMEM((groups, own_bands, lanes), jnp.float32),
            pltpu.VMEM((groups, own_bands, lanes), jnp.float32),
            pltpu.VMEM((groups, own_bands, lanes), jnp.float32),
            pltpu.VMEM((own_bands, lanes), jnp.float32),
            pltpu.VMEM((pixes, own_bands, lanes), jnp.float32),
            pltpu.SemaphoreType.DMA((4,)),
            pltpu.SemaphoreType.DMA((chunks,)),
            pltpu.SemaphoreType.DMA((chunks, groups)),
            pltpu.SemaphoreType.DMA((chunks, groups)),
            pltpu.SemaphoreType.DMA((groups,)),
            pltpu.SemaphoreType.DMA((groups,)),
            pltpu.SemaphoreType.DMA((pixes,)),
            pltpu.SemaphoreType.DMA((pixes,)),
        ],
        compiler_params=pltpu.CompilerParams(
            collective_id=0, has_side_effects=True, vmem_limit_bytes=56 * 2**20
        ),
        cost_estimate=pl.CostEstimate(
            flops=2 * GROUPS * GROUP * frame_total * share_cols,
            bytes_accessed=4 * frame_total * share_cols,
            transcendentals=0,
        ),
        name="band_coherence",
    )(band_edges, frames, trig, tapers, combine, power)
    return result.reshape(own_bands, 2, TAPERS, TAPERS)


def solution(mesh):
    return jax.shard_map(
        local,
        mesh=mesh,
        in_specs=(P("tm", "pix"), P()),
        out_specs=P("tm", None, None, None),
        check_vma=False,
    )
```

```python
import functools
import math

import jax
import jax.numpy as jnp
import ml_dtypes
import numpy as np
from jax import lax
from jax.experimental import pallas as pl
from jax.experimental.pallas import tpu as pltpu
from jax.sharding import PartitionSpec as P

TAPERS = 8
NB = 384
NBANDS = 64
PAIRS = TAPERS * TAPERS
BINS = 8
TILE = 256
CHUNK = 256
GROUP = 2 * TAPERS * BINS
GROUPS = NB // BINS
ROWS = 2048
MESH = pl.DeviceIdType.MESH
HIGHEST = lax.Precision.HIGHEST


def tables(length):
    frames = np.arange(length)
    phase = (np.arange(NB)[:, None] * frames[None, :] % length) * (2.0 * math.pi / length)
    trig = np.stack([np.cos(phase), -np.sin(phase)]).reshape(2, GROUPS, BINS, length)
    trig = trig.transpose(1, 0, 2, 3).reshape(2 * NB, length).astype(np.float32)
    rate = np.pi * (np.arange(TAPERS) + 1.0) / (length + 1)
    tapers = math.sqrt(2.0 / (length + 1)) * np.sin(rate[:, None] * (frames + 1.0))
    combine = np.zeros((2 * TAPERS, 2 * TAPERS, BINS, 2 * PAIRS), np.float32)
    power = np.zeros((2 * PAIRS, 2, 2, TAPERS, TAPERS), np.float32)
    for k in range(TAPERS):
        for l in range(TAPERS):
            kl = k * TAPERS + l
            combine[2 * k, 2 * l, :, kl] = 1.0
            combine[2 * k + 1, 2 * l + 1, :, kl] = 1.0
            combine[2 * k + 1, 2 * l, :, PAIRS + kl] = 1.0
            combine[2 * k, 2 * l + 1, :, PAIRS + kl] = -1.0
            power[k * TAPERS + k, 0, :, k, l] = 1.0
            power[l * TAPERS + l, 1, :, k, l] = 1.0
    combine = combine.reshape(2 * TAPERS * GROUP, 2 * PAIRS).astype(ml_dtypes.bfloat16)
    return trig, tapers.astype(np.float32), combine, power.reshape(2 * PAIRS, 4 * PAIRS)


def split(value):
    high = value.astype(jnp.bfloat16)
    return high, (value - high.astype(jnp.float32)).astype(jnp.bfloat16)


def kernel(
    groups, pixes, total_pixels,
    edges_ref, frames_ref, trig_hbm, tapers_hbm, combine_hbm, power_hbm,
    out_ref,
    data, centered, table, cross, trig, tapers, combine, power, mask, counts,
    part, got_tm, share, got_pix,
    table_sem, local_sem, send_sem, recv_sem, send_tm, recv_tm, send_pix, recv_pix,
):
    me = lax.axis_index("tm")
    me_pix = lax.axis_index("pix")
    chunks, frame_total, cols = data.shape
    frames_dev = frame_total // groups
    share_cols = chunks * cols
    own_bands = NBANDS // groups
    tiles = frame_total // TILE
    half = groups // 2
    base = me // half * half
    mine = me - base
    across = list(range(half))
    beside = list(range(half + 1, groups))
    peers = across + beside

    def target_of(d):
        return (half - base if d < half else base) + lax.rem(mine + d, half)

    def source_of(d):
        return (half - base if d < half else base) + lax.rem(mine + groups - d, half)

    def rows_of(group):
        return pl.ds(pl.multiple_of(group * frames_dev, frames_dev), frames_dev)

    def columns_of(group, s):
        return pl.ds(pl.multiple_of(group * share_cols + s * cols, 128), cols)

    barrier = pltpu.get_barrier_semaphore()
    for d in peers:
        pl.semaphore_signal(
            barrier, inc=1, device_id=(target_of(d), me_pix), device_id_type=MESH
        )
    for d in range(1, pixes):
        pl.semaphore_signal(
            barrier, inc=1, device_id=(me, lax.rem(me_pix + d, pixes)), device_id_type=MESH
        )
    pl.semaphore_wait(barrier, groups - 1 + pixes - 1)

    def frame_copy(s, d):
        to = target_of(d)
        return pltpu.make_async_remote_copy(
            src_ref=frames_ref.at[:, columns_of(to, s)],
            dst_ref=data.at[s, rows_of(me), :],
            send_sem=send_sem.at[s, d],
            recv_sem=recv_sem.at[s, d],
            device_id=(to, me_pix),
            device_id_type=MESH,
        )

    def own_copy(s):
        return pltpu.make_async_copy(
            frames_ref.at[:, columns_of(me, s)], data.at[s, rows_of(me), :], local_sem.at[s]
        )

    def send(s, carry):
        for d in across:
            frame_copy(s, d).start()
        for near in (2 * s, 2 * s + 1):
            for d in beside:
                frame_copy(near, d).start()
            own_copy(near).start()
        return carry

    def send_across(s, carry):
        for d in across:
            frame_copy(s, d).start()
        return carry

    lax.fori_loop(0, chunks // 2, send, 0)
    lax.fori_loop(chunks // 2, chunks, send_across, 0)

    table_copies = [
        pltpu.make_async_copy(source, target, table_sem.at[i])
        for i, (source, target) in enumerate(
            [(trig_hbm, trig), (tapers_hbm, tapers), (combine_hbm, combine), (power_hbm, power)]
        )
    ]
    for copy in table_copies:
        copy.start()

    bin_ids = lax.broadcasted_iota(jnp.int32, (1, NB), 1)
    for b in range(NBANDS):
        inside = (bin_ids >= edges_ref[b]) & (bin_ids < edges_ref[b + 1])
        mask[b:b + 1, :] = jnp.where(inside, 1.0, 0.0)
        count = (edges_ref[b + 1] - edges_ref[b]).astype(jnp.float32)
        counts[b // own_bands, b % own_bands:b % own_bands + 1, :] = jnp.full(
            (1, 2 * PAIRS), count, jnp.float32
        )
    for copy in table_copies:
        copy.wait()
    cross[...] = jnp.zeros_like(cross)

    def fill(g, carry):
        waves = trig[pl.ds(pl.multiple_of(g * 2 * BINS, 2 * BINS), 2 * BINS), :]
        for k in range(TAPERS):
            rows = pl.ds(pl.multiple_of(g * GROUP + k * 2 * BINS, 2 * BINS), 2 * BINS)
            table[rows, :] = (waves * tapers[k:k + 1, :]).astype(jnp.bfloat16)
        return carry

    lax.fori_loop(0, GROUPS, fill, 0)

    def center(s, slot):
        own_copy(s).wait()
        for d in peers:
            source = source_of(d)
            pltpu.make_async_remote_copy(
                src_ref=frames_ref.at[:, columns_of(me, s)],
                dst_ref=data.at[s, rows_of(source), :],
                send_sem=send_sem.at[s, d],
                recv_sem=recv_sem.at[s, d],
                device_id=(source, me_pix),
                device_id_type=MESH,
            ).wait_recv()
        total = jnp.zeros((1, cols), jnp.float32)
        for i in range(tiles):
            block = data[s, i * TILE:(i + 1) * TILE, :].astype(jnp.float32)
            total = total + jnp.sum(block, axis=0, keepdims=True)
        mean = total * (1.0 / frame_total)
        for i in range(tiles):
            block = data[s, i * TILE:(i + 1) * TILE, :].astype(jnp.float32)
            block = (block - mean).astype(jnp.bfloat16)
            centered[i * TILE:(i + 1) * TILE, slot * cols:(slot + 1) * cols] = block

    def accumulate(width):
        def transform(r, carry):
            rows = pl.ds(pl.multiple_of(r * ROWS, ROWS), ROWS)
            spectra = jnp.dot(
                table[rows, :], centered[:, :width], preferred_element_type=jnp.float32
            ).astype(jnp.bfloat16)
            for g in range(ROWS // GROUP // 2):
                block = spectra[2 * g * GROUP:2 * (g + 1) * GROUP]
                product = lax.dot_general(
                    block, block, (((1,), (1,)), ((), ())), preferred_element_type=jnp.float32
                )
                first = r * (ROWS // GROUP) + 2 * g
                cross[first] += product[:GROUP, :GROUP]
                cross[first + 1] += product[GROUP:, GROUP:]
            return carry

        lax.fori_loop(0, GROUPS * GROUP // ROWS, transform, 0)

    def pair(p, carry):
        center(2 * p, 0)
        center(2 * p + 1, 1)
        accumulate(2 * cols)
        return carry

    lax.fori_loop(0, chunks // 2 - 1, pair, 0)

    def single(s, carry):
        center(s, 0)
        accumulate(cols)
        return carry

    lax.fori_loop(chunks - 2, chunks, single, 0)

    band_mask = mask[...].astype(jnp.bfloat16)
    same_bin = (
        lax.broadcasted_iota(jnp.int32, (BINS, GROUP), 1) % BINS
        == lax.broadcasted_iota(jnp.int32, (BINS, GROUP), 0)
    )
    pieces = []
    for a in range(0, 2 * TAPERS, 2):
        sides = []
        for row in (a, a + 1):
            side = jnp.where(same_bin[None], cross[:, row * BINS:(row + 1) * BINS, :], 0.0)
            sides.append(side.reshape(NB, GROUP))
        high, low = split(jnp.concatenate(sides, axis=1))
        pieces.append(
            jnp.dot(band_mask, high, preferred_element_type=jnp.float32)
            + jnp.dot(band_mask, low, preferred_element_type=jnp.float32)
        )
    high, low = split(jnp.concatenate(pieces, axis=1))
    both = jnp.dot(
        jnp.concatenate([high, low], axis=0), combine[...], preferred_element_type=jnp.float32
    )
    both = both[:NBANDS] + both[NBANDS:]
    for g in range(groups):
        part[g] = both[g * own_bands:(g + 1) * own_bands, :]

    def band_copy(d, target, slot):
        return pltpu.make_async_remote_copy(
            src_ref=part.at[target],
            dst_ref=got_tm.at[slot],
            send_sem=send_tm.at[d],
            recv_sem=recv_tm.at[d],
            device_id=(target, me_pix),
            device_id_type=MESH,
        )

    for d in peers:
        band_copy(d, target_of(d), me).start()
    got_tm[me] = part[me]
    for d in peers:
        source = source_of(d)
        band_copy(d, source, source).wait_recv()
    value = got_tm[0]
    for g in range(1, groups):
        value = value + got_tm[g]
    share[...] = value
    got_pix[me_pix] = value

    def share_copy(d, target, slot):
        return pltpu.make_async_remote_copy(
            src_ref=share,
            dst_ref=got_pix.at[slot],
            send_sem=send_pix.at[d],
            recv_sem=recv_pix.at[d],
            device_id=(me, target),
            device_id_type=MESH,
        )

    for d in range(1, pixes):
        share_copy(d, lax.rem(me_pix + d, pixes), me_pix).start()
    for d in range(1, pixes):
        source = lax.rem(me_pix + pixes - d, pixes)
        share_copy(d, source, source).wait_recv()
    value = got_pix[0]
    for g in range(1, pixes):
        value = value + got_pix[g]

    powers = jnp.dot(value, power[...], precision=HIGHEST, preferred_element_type=jnp.float32)
    power_k = powers[:, :2 * PAIRS] + 1e-6
    power_l = powers[:, 2 * PAIRS:] + 1e-6
    lane = lax.broadcasted_iota(jnp.int32, value.shape, 1) % PAIRS
    off_diagonal = jnp.where(lane // TAPERS == lane % TAPERS, 0.0, 1.0)
    scaling = jnp.sqrt(counts[me] * total_pixels)
    out_ref[...] = value * (scaling * off_diagonal / jnp.sqrt(power_k * power_l))

    def drain(s, carry):
        for d in peers:
            frame_copy(s, d).wait_send()
        return carry

    lax.fori_loop(0, chunks, drain, 0)
    for d in peers:
        band_copy(d, target_of(d), me).wait_send()
    for d in range(1, pixes):
        share_copy(d, lax.rem(me_pix + d, pixes), me_pix).wait_send()


def local(frames, band_edges):
    groups = lax.axis_size("tm")
    pixes = lax.axis_size("pix")
    frames_dev, pix_dev = frames.shape
    frame_total = frames_dev * groups
    share_cols = pix_dev // groups
    cols = min(CHUNK, share_cols)
    chunks = share_cols // cols
    own_bands = NBANDS // groups
    trig, tapers, combine, power = tables(frame_total)
    anywhere = pl.BlockSpec(memory_space=pl.ANY)
    lanes = 2 * PAIRS
    result = pl.pallas_call(
        functools.partial(kernel, groups, pixes, float(pix_dev * pixes)),
        out_shape=jax.ShapeDtypeStruct((own_bands, lanes), jnp.float32),
        in_specs=[pl.BlockSpec(memory_space=pltpu.SMEM)] + [anywhere] * 5,
        out_specs=pl.BlockSpec(memory_space=pltpu.VMEM),
        scratch_shapes=[
            pltpu.VMEM((chunks, frame_total, cols), jnp.bfloat16),
            pltpu.VMEM((frame_total, 2 * cols), jnp.bfloat16),
            pltpu.VMEM((GROUPS * GROUP, frame_total), jnp.bfloat16),
            pltpu.VMEM((GROUPS, GROUP, GROUP), jnp.float32),
            pltpu.VMEM(trig.shape, jnp.float32),
            pltpu.VMEM(tapers.shape, jnp.float32),
            pltpu.VMEM(combine.shape, jnp.bfloat16),
            pltpu.VMEM(power.shape, jnp.float32),
            pltpu.VMEM((NBANDS, NB), jnp.float32),
            pltpu.VMEM((groups, own_bands, lanes), jnp.float32),
            pltpu.VMEM((groups, own_bands, lanes), jnp.float32),
            pltpu.VMEM((groups, own_bands, lanes), jnp.float32),
            pltpu.VMEM((own_bands, lanes), jnp.float32),
            pltpu.VMEM((pixes, own_bands, lanes), jnp.float32),
            pltpu.SemaphoreType.DMA((4,)),
            pltpu.SemaphoreType.DMA((chunks,)),
            pltpu.SemaphoreType.DMA((chunks, groups)),
            pltpu.SemaphoreType.DMA((chunks, groups)),
            pltpu.SemaphoreType.DMA((groups,)),
            pltpu.SemaphoreType.DMA((groups,)),
            pltpu.SemaphoreType.DMA((pixes,)),
            pltpu.SemaphoreType.DMA((pixes,)),
        ],
        compiler_params=pltpu.CompilerParams(
            collective_id=0, has_side_effects=True, vmem_limit_bytes=56 * 2**20
        ),
        cost_estimate=pl.CostEstimate(
            flops=2 * GROUPS * GROUP * frame_total * share_cols,
            bytes_accessed=4 * frame_total * share_cols,
            transcendentals=0,
        ),
        name="band_coherence",
    )(band_edges, frames, trig, tapers, combine, power)
    return result.reshape(own_bands, 2, TAPERS, TAPERS)


def solution(mesh):
    return jax.shard_map(
        local,
        mesh=mesh,
        in_specs=(P("tm", "pix"), P()),
        out_specs=P("tm", None, None, None),
        check_vma=False,
    )
```

```python
import functools
import math

import jax
import jax.numpy as jnp
import ml_dtypes
import numpy as np
from jax import lax
from jax.experimental import pallas as pl
from jax.experimental.pallas import tpu as pltpu
from jax.sharding import PartitionSpec as P

TAPERS = 8
NB = 384
NBANDS = 64
PAIRS = TAPERS * TAPERS
BINS = 8
TILE = 256
CHUNK = 512
GROUP = 2 * TAPERS * BINS
GROUPS = NB // BINS
ROWS = 2048
MESH = pl.DeviceIdType.MESH
HIGHEST = lax.Precision.HIGHEST


def tables(length):
    frames = np.arange(length)
    phase = (np.arange(NB)[:, None] * frames[None, :] % length) * (2.0 * math.pi / length)
    trig = np.stack([np.cos(phase), -np.sin(phase)]).reshape(2, GROUPS, BINS, length)
    trig = trig.transpose(1, 0, 2, 3).reshape(2 * NB, length).astype(np.float32)
    rate = np.pi * (np.arange(TAPERS) + 1.0) / (length + 1)
    tapers = math.sqrt(2.0 / (length + 1)) * np.sin(rate[:, None] * (frames + 1.0))
    combine = np.zeros((2 * TAPERS, 2 * TAPERS, BINS, 2 * PAIRS), np.float32)
    power = np.zeros((2 * PAIRS, 2, 2, TAPERS, TAPERS), np.float32)
    for k in range(TAPERS):
        for l in range(TAPERS):
            kl = k * TAPERS + l
            combine[2 * k, 2 * l, :, kl] = 1.0
            combine[2 * k + 1, 2 * l + 1, :, kl] = 1.0
            combine[2 * k + 1, 2 * l, :, PAIRS + kl] = 1.0
            combine[2 * k, 2 * l + 1, :, PAIRS + kl] = -1.0
            power[k * TAPERS + k, 0, :, k, l] = 1.0
            power[l * TAPERS + l, 1, :, k, l] = 1.0
    combine = combine.reshape(2 * TAPERS * GROUP, 2 * PAIRS).astype(ml_dtypes.bfloat16)
    return trig, tapers.astype(np.float32), combine, power.reshape(2 * PAIRS, 4 * PAIRS)


def split(value):
    high = value.astype(jnp.bfloat16)
    return high, (value - high.astype(jnp.float32)).astype(jnp.bfloat16)


def kernel(
    groups, pixes, total_pixels,
    edges_ref, frames_ref, trig_hbm, tapers_hbm, combine_hbm, power_hbm,
    out_ref,
    data, centered, table, cross, trig, tapers, combine, power, mask, counts,
    part, got_tm, share, got_pix,
    table_sem, local_sem, send_sem, recv_sem, send_tm, recv_tm, send_pix, recv_pix,
):
    me = lax.axis_index("tm")
    me_pix = lax.axis_index("pix")
    chunks, frame_total, cols = data.shape
    frames_dev = frame_total // groups
    share_cols = chunks * cols
    last = chunks - 1
    narrow = cols // 2
    own_bands = NBANDS // groups
    tiles = frame_total // TILE
    half = groups // 2
    base = me // half * half
    mine = me - base
    across = list(range(half))
    beside = list(range(half + 1, groups))
    peers = across + beside

    def target_of(d):
        return (half - base if d < half else base) + lax.rem(mine + d, half)

    def source_of(d):
        return (half - base if d < half else base) + lax.rem(mine + groups - d, half)

    def rows_of(group):
        return pl.ds(pl.multiple_of(group * frames_dev, frames_dev), frames_dev)

    def columns_of(group, piece):
        block, side = piece
        start = group * share_cols + block * cols
        if side is None:
            return pl.ds(pl.multiple_of(start, 128), cols)
        return pl.ds(pl.multiple_of(start + side * narrow, 128), narrow)

    def place_of(group, piece):
        block, side = piece
        if side is None:
            return data.at[block, rows_of(group), :]
        return data.at[block, rows_of(group), side * narrow:(side + 1) * narrow]

    def slot_of(piece):
        block, side = piece
        return block if side is None else last + side

    barrier = pltpu.get_barrier_semaphore()
    for d in peers:
        pl.semaphore_signal(
            barrier, inc=1, device_id=(target_of(d), me_pix), device_id_type=MESH
        )
    for d in range(1, pixes):
        pl.semaphore_signal(
            barrier, inc=1, device_id=(me, lax.rem(me_pix + d, pixes)), device_id_type=MESH
        )
    pl.semaphore_wait(barrier, groups - 1 + pixes - 1)

    def frame_copy(piece, d):
        to = target_of(d)
        return pltpu.make_async_remote_copy(
            src_ref=frames_ref.at[:, columns_of(to, piece)],
            dst_ref=place_of(me, piece),
            send_sem=send_sem.at[slot_of(piece), d],
            recv_sem=recv_sem.at[slot_of(piece), d],
            device_id=(to, me_pix),
            device_id_type=MESH,
        )

    def own_copy(piece):
        return pltpu.make_async_copy(
            frames_ref.at[:, columns_of(me, piece)], place_of(me, piece),
            local_sem.at[slot_of(piece)],
        )

    def send(piece):
        for d in peers:
            frame_copy(piece, d).start()
        own_copy(piece).start()

    def send_block(s, carry):
        send((s, None))
        return carry

    lax.fori_loop(0, last, send_block, 0)
    for side in range(2):
        send((last, side))

    table_copies = [
        pltpu.make_async_copy(source, target, table_sem.at[i])
        for i, (source, target) in enumerate(
            [(trig_hbm, trig), (tapers_hbm, tapers), (combine_hbm, combine), (power_hbm, power)]
        )
    ]
    for copy in table_copies:
        copy.start()

    bin_ids = lax.broadcasted_iota(jnp.int32, (1, NB), 1)
    for b in range(NBANDS):
        inside = (bin_ids >= edges_ref[b]) & (bin_ids < edges_ref[b + 1])
        mask[b:b + 1, :] = jnp.where(inside, 1.0, 0.0)
        count = (edges_ref[b + 1] - edges_ref[b]).astype(jnp.float32)
        counts[b // own_bands, b % own_bands:b % own_bands + 1, :] = jnp.full(
            (1, 2 * PAIRS), count, jnp.float32
        )
    for copy in table_copies:
        copy.wait()
    cross[...] = jnp.zeros_like(cross)

    def fill(g, carry):
        waves = trig[pl.ds(pl.multiple_of(g * 2 * BINS, 2 * BINS), 2 * BINS), :]
        for k in range(TAPERS):
            rows = pl.ds(pl.multiple_of(g * GROUP + k * 2 * BINS, 2 * BINS), 2 * BINS)
            table[rows, :] = (waves * tapers[k:k + 1, :]).astype(jnp.bfloat16)
        return carry

    lax.fori_loop(0, GROUPS, fill, 0)

    def center(piece):
        block, side = piece
        lanes = slice(0, cols) if side is None else slice(side * narrow, (side + 1) * narrow)
        width = cols if side is None else narrow
        own_copy(piece).wait()
        for d in peers:
            source = source_of(d)
            pltpu.make_async_remote_copy(
                src_ref=frames_ref.at[:, columns_of(me, piece)],
                dst_ref=place_of(source, piece),
                send_sem=send_sem.at[slot_of(piece), d],
                recv_sem=recv_sem.at[slot_of(piece), d],
                device_id=(source, me_pix),
                device_id_type=MESH,
            ).wait_recv()
        total = jnp.zeros((1, width), jnp.float32)
        for i in range(tiles):
            values = data[block, i * TILE:(i + 1) * TILE, lanes].astype(jnp.float32)
            total = total + jnp.sum(values, axis=0, keepdims=True)
        mean = total * (1.0 / frame_total)
        for i in range(tiles):
            values = data[block, i * TILE:(i + 1) * TILE, lanes].astype(jnp.float32)
            centered[i * TILE:(i + 1) * TILE, :width] = (values - mean).astype(jnp.bfloat16)

    def accumulate(width):
        def transform(r, carry):
            rows = pl.ds(pl.multiple_of(r * ROWS, ROWS), ROWS)
            spectra = jnp.dot(
                table[rows, :], centered[:, :width], preferred_element_type=jnp.float32
            ).astype(jnp.bfloat16)
            for g in range(ROWS // GROUP // 2):
                block = spectra[2 * g * GROUP:2 * (g + 1) * GROUP]
                product = lax.dot_general(
                    block, block, (((1,), (1,)), ((), ())), preferred_element_type=jnp.float32
                )
                first = r * (ROWS // GROUP) + 2 * g
                cross[first] += product[:GROUP, :GROUP]
                cross[first + 1] += product[GROUP:, GROUP:]
            return carry

        lax.fori_loop(0, GROUPS * GROUP // ROWS, transform, 0)

    def whole_block(s, carry):
        center((s, None))
        accumulate(cols)
        return carry

    lax.fori_loop(0, last, whole_block, 0)
    for side in range(2):
        center((last, side))
        accumulate(narrow)

    band_mask = mask[...].astype(jnp.bfloat16)
    same_bin = (
        lax.broadcasted_iota(jnp.int32, (BINS, GROUP), 1) % BINS
        == lax.broadcasted_iota(jnp.int32, (BINS, GROUP), 0)
    )
    pieces = []
    for a in range(0, 2 * TAPERS, 2):
        sides = []
        for row in (a, a + 1):
            side = jnp.where(same_bin[None], cross[:, row * BINS:(row + 1) * BINS, :], 0.0)
            sides.append(side.reshape(NB, GROUP))
        sides = jnp.concatenate(sides, axis=1).astype(jnp.bfloat16)
        pieces.append(jnp.dot(band_mask, sides, preferred_element_type=jnp.float32))
    high, low = split(jnp.concatenate(pieces, axis=1))
    both = jnp.dot(
        jnp.concatenate([high, low], axis=0), combine[...], preferred_element_type=jnp.float32
    )
    both = both[:NBANDS] + both[NBANDS:]
    for g in range(groups):
        part[g] = both[g * own_bands:(g + 1) * own_bands, :]

    def band_copy(d, target, slot):
        return pltpu.make_async_remote_copy(
            src_ref=part.at[target],
            dst_ref=got_tm.at[slot],
            send_sem=send_tm.at[d],
            recv_sem=recv_tm.at[d],
            device_id=(target, me_pix),
            device_id_type=MESH,
        )

    for d in peers:
        band_copy(d, target_of(d), me).start()
    got_tm[me] = part[me]
    for d in peers:
        source = source_of(d)
        band_copy(d, source, source).wait_recv()
    value = got_tm[0]
    for g in range(1, groups):
        value = value + got_tm[g]
    share[...] = value
    got_pix[me_pix] = value

    def share_copy(d, target, slot):
        return pltpu.make_async_remote_copy(
            src_ref=share,
            dst_ref=got_pix.at[slot],
            send_sem=send_pix.at[d],
            recv_sem=recv_pix.at[d],
            device_id=(me, target),
            device_id_type=MESH,
        )

    for d in range(1, pixes):
        share_copy(d, lax.rem(me_pix + d, pixes), me_pix).start()
    for d in range(1, pixes):
        source = lax.rem(me_pix + pixes - d, pixes)
        share_copy(d, source, source).wait_recv()
    value = got_pix[0]
    for g in range(1, pixes):
        value = value + got_pix[g]

    powers = jnp.dot(value, power[...], precision=HIGHEST, preferred_element_type=jnp.float32)
    power_k = powers[:, :2 * PAIRS] + 1e-6
    power_l = powers[:, 2 * PAIRS:] + 1e-6
    lane = lax.broadcasted_iota(jnp.int32, value.shape, 1) % PAIRS
    off_diagonal = jnp.where(lane // TAPERS == lane % TAPERS, 0.0, 1.0)
    scaling = jnp.sqrt(counts[me] * total_pixels)
    out_ref[...] = value * (scaling * off_diagonal / jnp.sqrt(power_k * power_l))

    def drain(s, carry):
        for d in peers:
            frame_copy((s, None), d).wait_send()
        return carry

    lax.fori_loop(0, last, drain, 0)
    for side in range(2):
        for d in peers:
            frame_copy((last, side), d).wait_send()
    for d in peers:
        band_copy(d, target_of(d), me).wait_send()
    for d in range(1, pixes):
        share_copy(d, lax.rem(me_pix + d, pixes), me_pix).wait_send()


def local(frames, band_edges):
    groups = lax.axis_size("tm")
    pixes = lax.axis_size("pix")
    frames_dev, pix_dev = frames.shape
    frame_total = frames_dev * groups
    share_cols = pix_dev // groups
    cols = min(CHUNK, share_cols)
    chunks = share_cols // cols
    own_bands = NBANDS // groups
    trig, tapers, combine, power = tables(frame_total)
    anywhere = pl.BlockSpec(memory_space=pl.ANY)
    lanes = 2 * PAIRS
    result = pl.pallas_call(
        functools.partial(kernel, groups, pixes, float(pix_dev * pixes)),
        out_shape=jax.ShapeDtypeStruct((own_bands, lanes), jnp.float32),
        in_specs=[pl.BlockSpec(memory_space=pltpu.SMEM)] + [anywhere] * 5,
        out_specs=pl.BlockSpec(memory_space=pltpu.VMEM),
        scratch_shapes=[
            pltpu.VMEM((chunks, frame_total, cols), jnp.bfloat16),
            pltpu.VMEM((frame_total, cols), jnp.bfloat16),
            pltpu.VMEM((GROUPS * GROUP, frame_total), jnp.bfloat16),
            pltpu.VMEM((GROUPS, GROUP, GROUP), jnp.float32),
            pltpu.VMEM(trig.shape, jnp.float32),
            pltpu.VMEM(tapers.shape, jnp.float32),
            pltpu.VMEM(combine.shape, jnp.bfloat16),
            pltpu.VMEM(power.shape, jnp.float32),
            pltpu.VMEM((NBANDS, NB), jnp.float32),
            pltpu.VMEM((groups, own_bands, lanes), jnp.float32),
            pltpu.VMEM((groups, own_bands, lanes), jnp.float32),
            pltpu.VMEM((groups, own_bands, lanes), jnp.float32),
            pltpu.VMEM((own_bands, lanes), jnp.float32),
            pltpu.VMEM((pixes, own_bands, lanes), jnp.float32),
            pltpu.SemaphoreType.DMA((4,)),
            pltpu.SemaphoreType.DMA((chunks + 1,)),
            pltpu.SemaphoreType.DMA((chunks + 1, groups)),
            pltpu.SemaphoreType.DMA((chunks + 1, groups)),
            pltpu.SemaphoreType.DMA((groups,)),
            pltpu.SemaphoreType.DMA((groups,)),
            pltpu.SemaphoreType.DMA((pixes,)),
            pltpu.SemaphoreType.DMA((pixes,)),
        ],
        compiler_params=pltpu.CompilerParams(
            collective_id=0, has_side_effects=True, vmem_limit_bytes=56 * 2**20
        ),
        cost_estimate=pl.CostEstimate(
            flops=2 * GROUPS * GROUP * frame_total * share_cols,
            bytes_accessed=4 * frame_total * share_cols,
            transcendentals=0,
        ),
        name="band_coherence",
    )(band_edges, frames, trig, tapers, combine, power)
    return result.reshape(own_bands, 2, TAPERS, TAPERS)


def solution(mesh):
    return jax.shard_map(
        local,
        mesh=mesh,
        in_specs=(P("tm", "pix"), P()),
        out_specs=P("tm", None, None, None),
        check_vma=False,
    )
```

```python
import functools
import math

import jax
import jax.numpy as jnp
import ml_dtypes
import numpy as np
from jax import lax
from jax.experimental import pallas as pl
from jax.experimental.pallas import tpu as pltpu
from jax.sharding import PartitionSpec as P

TAPERS = 8
NB = 384
NBANDS = 64
PAIRS = TAPERS * TAPERS
BINS = 8
TILE = 256
CHUNK = 512
WINDOW = 2
GROUP = 2 * TAPERS * BINS
GROUPS = NB // BINS
ROWS = 2048
MESH = pl.DeviceIdType.MESH
HIGHEST = lax.Precision.HIGHEST


def tables(length):
    frames = np.arange(length)
    phase = (np.arange(NB)[:, None] * frames[None, :] % length) * (2.0 * math.pi / length)
    trig = np.stack([np.cos(phase), -np.sin(phase)]).reshape(2, GROUPS, BINS, length)
    trig = trig.transpose(1, 0, 2, 3).reshape(2 * NB, length).astype(np.float32)
    rate = np.pi * (np.arange(TAPERS) + 1.0) / (length + 1)
    tapers = math.sqrt(2.0 / (length + 1)) * np.sin(rate[:, None] * (frames + 1.0))
    combine = np.zeros((2 * TAPERS, 2 * TAPERS, BINS, 2 * PAIRS), np.float32)
    power = np.zeros((2 * PAIRS, 2, 2, TAPERS, TAPERS), np.float32)
    for k in range(TAPERS):
        for l in range(TAPERS):
            kl = k * TAPERS + l
            combine[2 * k, 2 * l, :, kl] = 1.0
            combine[2 * k + 1, 2 * l + 1, :, kl] = 1.0
            combine[2 * k + 1, 2 * l, :, PAIRS + kl] = 1.0
            combine[2 * k, 2 * l + 1, :, PAIRS + kl] = -1.0
            power[k * TAPERS + k, 0, :, k, l] = 1.0
            power[l * TAPERS + l, 1, :, k, l] = 1.0
    combine = combine.reshape(2 * TAPERS * GROUP, 2 * PAIRS).astype(ml_dtypes.bfloat16)
    return trig, tapers.astype(np.float32), combine, power.reshape(2 * PAIRS, 4 * PAIRS)


def split(value):
    high = value.astype(jnp.bfloat16)
    return high, (value - high.astype(jnp.float32)).astype(jnp.bfloat16)


def kernel(
    groups, pixes, total_pixels,
    edges_ref, frames_ref, trig_hbm, tapers_hbm, combine_hbm, power_hbm,
    out_ref,
    data, centered, table, cross, trig, tapers, combine, power, mask, counts,
    part, got_tm, share, got_pix,
    table_sem, local_sem, send_sem, recv_sem, send_tm, recv_tm, send_pix, recv_pix,
):
    me = lax.axis_index("tm")
    me_pix = lax.axis_index("pix")
    chunks, frame_total, cols = data.shape
    frames_dev = frame_total // groups
    share_cols = chunks * cols
    last = chunks - 1
    narrow = cols // 2
    own_bands = NBANDS // groups
    tiles = frame_total // TILE
    half = groups // 2
    base = me // half * half
    mine = me - base
    across = list(range(half))
    beside = list(range(half + 1, groups))
    peers = across + beside

    def target_of(d):
        return (half - base if d < half else base) + lax.rem(mine + d, half)

    def source_of(d):
        return (half - base if d < half else base) + lax.rem(mine + groups - d, half)

    def rows_of(group):
        return pl.ds(pl.multiple_of(group * frames_dev, frames_dev), frames_dev)

    def columns_of(group, piece):
        block, side = piece
        start = group * share_cols + block * cols
        if side is None:
            return pl.ds(pl.multiple_of(start, 128), cols)
        return pl.ds(pl.multiple_of(start + side * narrow, 128), narrow)

    def place_of(group, piece):
        block, side = piece
        if side is None:
            return data.at[block, rows_of(group), :]
        return data.at[block, rows_of(group), side * narrow:(side + 1) * narrow]

    def slot_of(piece):
        block, side = piece
        return block if side is None else last + side

    barrier = pltpu.get_barrier_semaphore()
    for d in peers:
        pl.semaphore_signal(
            barrier, inc=1, device_id=(target_of(d), me_pix), device_id_type=MESH
        )
    for d in range(1, pixes):
        pl.semaphore_signal(
            barrier, inc=1, device_id=(me, lax.rem(me_pix + d, pixes)), device_id_type=MESH
        )
    pl.semaphore_wait(barrier, groups - 1 + pixes - 1)

    def frame_copy(piece, d):
        to = target_of(d)
        return pltpu.make_async_remote_copy(
            src_ref=frames_ref.at[:, columns_of(to, piece)],
            dst_ref=place_of(me, piece),
            send_sem=send_sem.at[slot_of(piece), d],
            recv_sem=recv_sem.at[slot_of(piece), d],
            device_id=(to, me_pix),
            device_id_type=MESH,
        )

    def own_copy(piece):
        return pltpu.make_async_copy(
            frames_ref.at[:, columns_of(me, piece)], place_of(me, piece),
            local_sem.at[slot_of(piece)],
        )

    def send(piece):
        for d in peers:
            frame_copy(piece, d).start()
        own_copy(piece).start()

    def send_block(s, carry):
        send((s, None))
        return carry

    def send_halves():
        for side in range(2):
            send((last, side))

    ahead = min(WINDOW, last)
    lax.fori_loop(0, ahead, send_block, 0)
    if last == 0:
        send_halves()

    table_copies = [
        pltpu.make_async_copy(source, target, table_sem.at[i])
        for i, (source, target) in enumerate(
            [(trig_hbm, trig), (tapers_hbm, tapers), (combine_hbm, combine), (power_hbm, power)]
        )
    ]
    for copy in table_copies:
        copy.start()

    bin_ids = lax.broadcasted_iota(jnp.int32, (1, NB), 1)
    for b in range(NBANDS):
        inside = (bin_ids >= edges_ref[b]) & (bin_ids < edges_ref[b + 1])
        mask[b:b + 1, :] = jnp.where(inside, 1.0, 0.0)
        count = (edges_ref[b + 1] - edges_ref[b]).astype(jnp.float32)
        counts[b // own_bands, b % own_bands:b % own_bands + 1, :] = jnp.full(
            (1, 2 * PAIRS), count, jnp.float32
        )
    for copy in table_copies:
        copy.wait()
    cross[...] = jnp.zeros_like(cross)

    def fill(g, carry):
        waves = trig[pl.ds(pl.multiple_of(g * 2 * BINS, 2 * BINS), 2 * BINS), :]
        for k in range(TAPERS):
            rows = pl.ds(pl.multiple_of(g * GROUP + k * 2 * BINS, 2 * BINS), 2 * BINS)
            table[rows, :] = (waves * tapers[k:k + 1, :]).astype(jnp.bfloat16)
        return carry

    lax.fori_loop(0, GROUPS, fill, 0)

    def center(piece):
        block, side = piece
        lanes = slice(0, cols) if side is None else slice(side * narrow, (side + 1) * narrow)
        width = cols if side is None else narrow
        own_copy(piece).wait()
        for d in peers:
            source = source_of(d)
            pltpu.make_async_remote_copy(
                src_ref=frames_ref.at[:, columns_of(me, piece)],
                dst_ref=place_of(source, piece),
                send_sem=send_sem.at[slot_of(piece), d],
                recv_sem=recv_sem.at[slot_of(piece), d],
                device_id=(source, me_pix),
                device_id_type=MESH,
            ).wait_recv()
        total = jnp.zeros((1, width), jnp.float32)
        for i in range(tiles):
            values = data[block, i * TILE:(i + 1) * TILE, lanes].astype(jnp.float32)
            total = total + jnp.sum(values, axis=0, keepdims=True)
        mean = total * (1.0 / frame_total)
        for i in range(tiles):
            values = data[block, i * TILE:(i + 1) * TILE, lanes].astype(jnp.float32)
            centered[i * TILE:(i + 1) * TILE, :width] = (values - mean).astype(jnp.bfloat16)

    def accumulate(width):
        def transform(r, carry):
            rows = pl.ds(pl.multiple_of(r * ROWS, ROWS), ROWS)
            spectra = jnp.dot(
                table[rows, :], centered[:, :width], preferred_element_type=jnp.float32
            ).astype(jnp.bfloat16)
            for g in range(ROWS // GROUP // 2):
                block = spectra[2 * g * GROUP:2 * (g + 1) * GROUP]
                product = lax.dot_general(
                    block, block, (((1,), (1,)), ((), ())), preferred_element_type=jnp.float32
                )
                first = r * (ROWS // GROUP) + 2 * g
                cross[first] += product[:GROUP, :GROUP]
                cross[first + 1] += product[GROUP:, GROUP:]
            return carry

        lax.fori_loop(0, GROUPS * GROUP // ROWS, transform, 0)

    def whole_block(s, carry):
        center((s, None))
        if carry is None:
            send_halves()
        elif carry is not False:
            send_block(s + ahead, carry)
        accumulate(cols)
        return carry

    if last > 0:
        lax.fori_loop(0, last - ahead, whole_block, 0)
        whole_block(last - ahead, None)
        for s in range(last - ahead + 1, last):
            whole_block(s, False)
    for side in range(2):
        center((last, side))
        accumulate(narrow)

    band_mask = mask[...].astype(jnp.bfloat16)
    same_bin = (
        lax.broadcasted_iota(jnp.int32, (BINS, GROUP), 1) % BINS
        == lax.broadcasted_iota(jnp.int32, (BINS, GROUP), 0)
    )
    pieces = []
    for a in range(0, 2 * TAPERS, 2):
        sides = []
        for row in (a, a + 1):
            side = jnp.where(same_bin[None], cross[:, row * BINS:(row + 1) * BINS, :], 0.0)
            sides.append(side.reshape(NB, GROUP))
        sides = jnp.concatenate(sides, axis=1).astype(jnp.bfloat16)
        pieces.append(jnp.dot(band_mask, sides, preferred_element_type=jnp.float32))
    high, low = split(jnp.concatenate(pieces, axis=1))
    both = jnp.dot(
        jnp.concatenate([high, low], axis=0), combine[...], preferred_element_type=jnp.float32
    )
    both = both[:NBANDS] + both[NBANDS:]
    for g in range(groups):
        part[g] = both[g * own_bands:(g + 1) * own_bands, :]

    def band_copy(d, target, slot):
        return pltpu.make_async_remote_copy(
            src_ref=part.at[target],
            dst_ref=got_tm.at[slot],
            send_sem=send_tm.at[d],
            recv_sem=recv_tm.at[d],
            device_id=(target, me_pix),
            device_id_type=MESH,
        )

    for d in peers:
        band_copy(d, target_of(d), me).start()
    got_tm[me] = part[me]
    for d in peers:
        source = source_of(d)
        band_copy(d, source, source).wait_recv()
    value = got_tm[0]
    for g in range(1, groups):
        value = value + got_tm[g]
    share[...] = value
    got_pix[me_pix] = value

    def share_copy(d, target, slot):
        return pltpu.make_async_remote_copy(
            src_ref=share,
            dst_ref=got_pix.at[slot],
            send_sem=send_pix.at[d],
            recv_sem=recv_pix.at[d],
            device_id=(me, target),
            device_id_type=MESH,
        )

    for d in range(1, pixes):
        share_copy(d, lax.rem(me_pix + d, pixes), me_pix).start()
    for d in range(1, pixes):
        source = lax.rem(me_pix + pixes - d, pixes)
        share_copy(d, source, source).wait_recv()
    value = got_pix[0]
    for g in range(1, pixes):
        value = value + got_pix[g]

    powers = jnp.dot(value, power[...], precision=HIGHEST, preferred_element_type=jnp.float32)
    power_k = powers[:, :2 * PAIRS] + 1e-6
    power_l = powers[:, 2 * PAIRS:] + 1e-6
    lane = lax.broadcasted_iota(jnp.int32, value.shape, 1) % PAIRS
    off_diagonal = jnp.where(lane // TAPERS == lane % TAPERS, 0.0, 1.0)
    scaling = jnp.sqrt(counts[me] * total_pixels)
    out_ref[...] = value * (scaling * off_diagonal / jnp.sqrt(power_k * power_l))

    def drain(s, carry):
        for d in peers:
            frame_copy((s, None), d).wait_send()
        return carry

    lax.fori_loop(0, last, drain, 0)
    for side in range(2):
        for d in peers:
            frame_copy((last, side), d).wait_send()
    for d in peers:
        band_copy(d, target_of(d), me).wait_send()
    for d in range(1, pixes):
        share_copy(d, lax.rem(me_pix + d, pixes), me_pix).wait_send()


def local(frames, band_edges):
    groups = lax.axis_size("tm")
    pixes = lax.axis_size("pix")
    frames_dev, pix_dev = frames.shape
    frame_total = frames_dev * groups
    share_cols = pix_dev // groups
    cols = min(CHUNK, share_cols)
    chunks = share_cols // cols
    own_bands = NBANDS // groups
    trig, tapers, combine, power = tables(frame_total)
    anywhere = pl.BlockSpec(memory_space=pl.ANY)
    lanes = 2 * PAIRS
    result = pl.pallas_call(
        functools.partial(kernel, groups, pixes, float(pix_dev * pixes)),
        out_shape=jax.ShapeDtypeStruct((own_bands, lanes), jnp.float32),
        in_specs=[pl.BlockSpec(memory_space=pltpu.SMEM)] + [anywhere] * 5,
        out_specs=pl.BlockSpec(memory_space=pltpu.VMEM),
        scratch_shapes=[
            pltpu.VMEM((chunks, frame_total, cols), jnp.bfloat16),
            pltpu.VMEM((frame_total, cols), jnp.bfloat16),
            pltpu.VMEM((GROUPS * GROUP, frame_total), jnp.bfloat16),
            pltpu.VMEM((GROUPS, GROUP, GROUP), jnp.float32),
            pltpu.VMEM(trig.shape, jnp.float32),
            pltpu.VMEM(tapers.shape, jnp.float32),
            pltpu.VMEM(combine.shape, jnp.bfloat16),
            pltpu.VMEM(power.shape, jnp.float32),
            pltpu.VMEM((NBANDS, NB), jnp.float32),
            pltpu.VMEM((groups, own_bands, lanes), jnp.float32),
            pltpu.VMEM((groups, own_bands, lanes), jnp.float32),
            pltpu.VMEM((groups, own_bands, lanes), jnp.float32),
            pltpu.VMEM((own_bands, lanes), jnp.float32),
            pltpu.VMEM((pixes, own_bands, lanes), jnp.float32),
            pltpu.SemaphoreType.DMA((4,)),
            pltpu.SemaphoreType.DMA((chunks + 1,)),
            pltpu.SemaphoreType.DMA((chunks + 1, groups)),
            pltpu.SemaphoreType.DMA((chunks + 1, groups)),
            pltpu.SemaphoreType.DMA((groups,)),
            pltpu.SemaphoreType.DMA((groups,)),
            pltpu.SemaphoreType.DMA((pixes,)),
            pltpu.SemaphoreType.DMA((pixes,)),
        ],
        compiler_params=pltpu.CompilerParams(
            collective_id=0, has_side_effects=True, vmem_limit_bytes=56 * 2**20
        ),
        cost_estimate=pl.CostEstimate(
            flops=2 * GROUPS * GROUP * frame_total * share_cols,
            bytes_accessed=4 * frame_total * share_cols,
            transcendentals=0,
        ),
        name="band_coherence",
    )(band_edges, frames, trig, tapers, combine, power)
    return result.reshape(own_bands, 2, TAPERS, TAPERS)


def solution(mesh):
    return jax.shard_map(
        local,
        mesh=mesh,
        in_specs=(P("tm", "pix"), P()),
        out_specs=P("tm", None, None, None),
        check_vma=False,
    )
```
